32 devices in a mesh: gx: 2 (over x), gy: 4 (over y, core), gz: 4 (over z).
Axes of the slice: x: 2, y: 2, z: 4, core: 2. Of those that a mesh axis runs over, the one named last changes fastest.
Arguments:
- source: float32 [32, 128, 512], P('gx', 'gz', 'gy'), may hold values from -24 to 24
- conductance: float32 [32, 128, 512], P('gx', 'gz', 'gy'), may hold values from 0.5 to 4
- field_start: float32 [32, 128, 512], P('gx', 'gz', 'gy'), may hold values from -4 to 4
- panel_cell: int32 [3, 1024], P(None, ('gx', 'gy', 'gz')), may hold values from 0 to 511, as said below
- panel_area: float32 [1024], P(('gx', 'gy', 'gz')), may hold values from 0.5 to 2
Outputs:
- field: float32 [32, 128, 512], P('gx', 'gz', 'gy')
- potential: float32 [1024], P(('gx', 'gy', 'gz'))
The draws below stay inside these ranges and needn't reach their ends.
Inputs may be any that keep to these rules, and one draw needn't show every extreme that they name: `panel_cell`: every column names a cell on the outer surface of the grid of 32 x 128 x 512 cells; several panels may share a cell; the panels are in no order of place.
All inputs are finite; a program needn't handle non-finite values.
Results may differ from the reference program's by a relative error of at most 0.0003.
Values sent between devices are 32-bit elements; how exact they have to be, the bound alone decides.
A program may use at most 64 MiB of HBM per device.

```python
import math
import jax
import jax.numpy as jnp
from jax import lax

ROUNDS = 2
SWEEPS = 4
NX = 32
NY = 128
NZ = 512
PANELS = 1024


def draw_panel_cell(key, part):
    key = jax.random.fold_in(key, 11)
    keys = jax.random.split(key, 5)
    face_axis = jax.random.randint(keys[0], (PANELS,), 0, 3)
    face_side = jax.random.randint(keys[1], (PANELS,), 0, 2)
    along_x = jax.random.randint(keys[2], (PANELS,), 0, NX)
    along_y = jax.random.randint(keys[3], (PANELS,), 0, NY)
    along_z = jax.random.randint(keys[4], (PANELS,), 0, NZ)
    along_x = jnp.where(face_axis == 0, face_side * (NX - 1), along_x)
    along_y = jnp.where(face_axis == 1, face_side * (NY - 1), along_y)
    along_z = jnp.where(face_axis == 2, face_side * (NZ - 1), along_z)
    along_x = along_x.at[0].set(NX - 1).at[1].set(0)
    along_y = along_y.at[0].set(NY - 1).at[1].set(0)
    along_z = along_z.at[0].set(NZ - 1).at[1].set(0)
    return jnp.stack([along_x, along_y, along_z], 0).astype(jnp.int32)


def steps_of(own_key, extent, shards, smallest, top_value):
    def one(dim, blocks):
        heights = jax.random.uniform(jax.random.fold_in(jax.random.fold_in(own_key, 6), dim), (blocks,), jnp.float32, smallest / len(shards), top_value / len(shards))
        return jnp.repeat(jnp.exp(heights), extent[dim] // blocks).reshape((-1,) + (1,) * (len(extent) - dim - 1))

    gain = one(*shards[0])
    for cut in shards[1:]:
        gain = gain * one(*cut)
    return gain


def gaussian(own_key, extent, deviation, limit, cuts=(), held_as=jnp.bfloat16):
    values = deviation * jax.random.normal(own_key, extent, jnp.float32)
    if cuts:
        values = values * steps_of(own_key, extent, cuts, -0.22, 0.18)
    return jnp.clip(values, -limit, limit).astype(held_as)


def setup_inputs(seed: int = 0) -> dict:
    key_of = jax.random.split(jax.random.key(seed), 6)
    source = gaussian(key_of[0], (NX, NY, NZ), 4.0, 24.0, ((0, 2), (1, 4), (2, 4)), jnp.float32)
    conductance = jnp.clip(jnp.exp(math.log(4.0) - 2.0794415 * jax.random.uniform(key_of[1], (NX, NY, NZ), jnp.float32) ** steps_of(key_of[1], (NX, NY, NZ), ((0, 2), (1, 4), (2, 4)), -0.2, 0.2)), 0.5, 4.0)
    field_start = gaussian(key_of[2], (NX, NY, NZ), 0.5, 4.0, ((0, 2), (1, 4), (2, 4)), jnp.float32)
    panel_cell = draw_panel_cell(jax.random.fold_in(key_of[5], 71), 0)
    panel_area = jnp.clip(jnp.exp(math.log(2.0) - 1.3862944 * jax.random.uniform(key_of[4], (PANELS,), jnp.float32) ** steps_of(key_of[4], (PANELS,), ((0, 32),), -0.2, 0.2)), 0.5, 2.0)
    return dict(source=source, conductance=conductance, field_start=field_start, panel_cell=panel_cell, panel_area=panel_area)


relax = 0.8

def neighbours(array):
    return [array[2:, 1:-1, 1:-1], array[:-2, 1:-1, 1:-1], array[1:-1, 2:, 1:-1], array[1:-1, :-2, 1:-1], array[1:-1, 1:-1, 2:], array[1:-1, 1:-1, :-2]]

def sweep(padded, coeff, load):
    center = padded[1:-1, 1:-1, 1:-1]
    middle = coeff[1:-1, 1:-1, 1:-1]
    diagonal = jnp.zeros_like(center)
    coupled = jnp.zeros_like(center)
    for value, other in zip(neighbours(padded), neighbours(coeff)):
        face_coeff = 0.5 * (middle + other)
        diagonal = diagonal + face_coeff
        coupled = coupled + face_coeff * value
    inside = middle > 0.0
    safe = jnp.where(inside, diagonal, 1.0)
    update = center + relax * (load - (diagonal * center - coupled)) / safe
    return jnp.where(inside, update, 0.0)

def block_kernel(targets, columns, weights):
    squared = jnp.zeros((targets.shape[1], columns.shape[1]), jnp.float32)
    for component in range(3):
        offset = targets[component][:, None] - columns[component][None, :]
        squared = squared + offset * offset
    kernel = lax.rsqrt(squared + 1.0)
    return jnp.dot(kernel, weights, precision=lax.Precision.HIGHEST)

def reference(source, conductance, field_start, panel_cell, panel_area):
    coords = panel_cell.astype(jnp.float32)
    count = coords.shape[1]
    row_blocks = coords.reshape(3, count // 128, 128).transpose(1, 0, 2)
    coeff = jnp.pad(conductance, 1)
    field = field_start
    potential = jnp.zeros((count,), jnp.float32)
    for repeat in range(ROUNDS):
        trace = field[panel_cell[0], panel_cell[1], panel_cell[2]]
        weights = panel_area * trace

        def row_potential(target_block):
            return block_kernel(target_block, coords, weights)
        potential = lax.map(row_potential, row_blocks).reshape(count)
        load = source.at[panel_cell[0], panel_cell[1], panel_cell[2]].add(potential)
        for sweep_index in range(SWEEPS):
            field = sweep(jnp.pad(field, 1), coeff, load)
    return (field, potential)
```

```python
import functools

import jax
import jax.numpy as jnp
from jax import lax
from jax.experimental import pallas as pl
from jax.experimental.pallas import tpu as pltpu
from jax.sharding import PartitionSpec as P

ROUNDS = 2
SWEEPS = 4
W = SWEEPS
relax = 0.8
MESH = pl.DeviceIdType.MESH
F32 = jnp.float32
BF16 = jnp.bfloat16


def split2(value):
    high = value.astype(BF16)
    low = (value - high.astype(F32)).astype(BF16)
    return high, low


def split3(value):
    high = value.astype(BF16)
    rest = value - high.astype(F32)
    mid = rest.astype(BF16)
    low = (rest - mid.astype(F32)).astype(BF16)
    return high, mid, low


def kernel(
    cfg, panel_ref, field_ref, source_ref, cond_ref, out_ref, pot_ref,
    ext, ext2, ping, pong, coef, inv, load, yrecv, yrecv2, zsend, zsend2, zrecv, zrecv2,
    ag1_send, ag1, ag_own, cells, ws1_send, ws1, ws2_send, ws2, cols, onehot, onehot_ext, spread, kmat,
    local_sem, ag1_ss, ag1_rs, ag2_ss, ag2_rs, h1_ss, h1_rs, h2_ss, h2_rs, w1_ss, w1_rs, w2_ss, w2_rs,
):
    gxn, gyn, gzn, sx, sy, sz, own, count = cfg
    q_count = gxn * gyn
    width = own * gzn
    ex, ey, ez = sx + 2 * W, sy + 8, 2 * sz
    rows = ex * ey
    rows_pad = zsend.shape[-1]
    gx, gy, gz = lax.axis_index("gx"), lax.axis_index("gy"), lax.axis_index("gz")
    q = gx * gyn + gy

    locals_ = []
    for a, ref in enumerate((field_ref, source_ref, cond_ref)):
        copy = pltpu.make_async_copy(ref, ext.at[a, W : W + sx, 0:sy, 0:sz], local_sem.at[a])
        copy.start()
        locals_.append(copy)

    for a in range(3):
        ext[a, 0:W, :, 0:sz] = jnp.zeros((W, ey, sz), F32)
        ext[a, W + sx :, :, 0:sz] = jnp.zeros((W, ey, sz), F32)
    ext2[0, 0:W, :, 0:sz] = jnp.zeros((W, ey, sz), F32)
    ext2[0, W + sx :, :, 0:sz] = jnp.zeros((W, ey, sz), F32)
    yrecv[...] = jnp.zeros(yrecv.shape, F32)
    yrecv2[...] = jnp.zeros(yrecv2.shape, F32)
    zrecv[...] = jnp.zeros(zrecv.shape, F32)
    zrecv2[...] = jnp.zeros(zrecv2.shape, F32)

    def z_peer(offset):
        return (gx, gy, lax.rem(gz + offset, gzn))

    def q_peer(offset):
        other = lax.rem(q + offset, q_count)
        return (other // gyn, lax.rem(other, gyn), gz)

    def in_grid(dx, dy):
        ok = None
        for step, index, size in ((dx, gx, gxn), (dy, gz, gzn)):
            if step:
                test = index < size - 1 if step > 0 else index > 0
                ok = test if ok is None else jnp.logical_and(ok, test)
        return ok

    barrier = pltpu.get_barrier_semaphore()
    total = jnp.int32(gzn - 1 + q_count - 1)
    for offset in range(1, gzn):
        pl.semaphore_signal(barrier, inc=1, device_id=z_peer(offset), device_id_type=MESH)
    for offset in range(1, q_count):
        pl.semaphore_signal(barrier, inc=1, device_id=q_peer(offset), device_id_type=MESH)
    for dx in (-1, 1):
        for dy in (-1, 1):
            ok = in_grid(dx, dy)
            total = total + jnp.where(ok, 1, 0).astype(jnp.int32)

            @pl.when(ok)
            def _():
                pl.semaphore_signal(barrier, inc=1, device_id=(gx + dx, gy, gz + dy), device_id_type=MESH)

    lane_w = lax.broadcasted_iota(jnp.int32, (8, width), 1)
    mine_lanes = jnp.logical_and(lane_w >= gz * own, lane_w < (gz + 1) * own)
    own_tile = jnp.where(mine_lanes, panel_ref[...], 0.0)
    ag1_send[...] = own_tile
    pl.semaphore_wait(barrier, total)

    def exchange_z(src, dst, ss, rs):
        copies = []
        for offset in range(1, gzn):
            copy = pltpu.make_async_remote_copy(
                src_ref=src, dst_ref=dst.at[offset - 1], send_sem=ss.at[offset - 1], recv_sem=rs.at[offset - 1],
                device_id=z_peer(offset), device_id_type=MESH,
            )
            copy.start()
            copies.append(copy)
        return copies

    ag1_copies = exchange_z(ag1_send, ag1, ag1_ss, ag1_rs)
    for copy in locals_:
        copy.wait()

    directions = [(dx, dy) for dx in (-1, 0, 1) for dy in (-1, 0, 1) if dx or dy]

    def halo_copies(base, yr, ss, rs):
        made = []
        for n, (dx, dy) in enumerate(directions):
            xs = {-1: pl.ds(W, W), 0: pl.ds(W, sx), 1: pl.ds(sx, W)}[dx]
            ys = {-1: pl.ds(0, 8), 0: pl.ds(0, sy), 1: pl.ds(sy - 8, 8)}[dy]
            xd = {-1: pl.ds(W + sx, W), 0: pl.ds(W, sx), 1: pl.ds(0, W)}[dx]
            src = base.at[:, xs, ys, pl.ds(0, sz)]
            if dy == 0:
                dst = base.at[:, xd, pl.ds(0, sy), pl.ds(0, sz)]
            else:
                dst = yr.at[0 if dy < 0 else 1, :, xd]
            made.append(
                (
                    pltpu.make_async_remote_copy(
                        src_ref=src, dst_ref=dst, send_sem=ss.at[n], recv_sem=rs.at[n],
                        device_id=(gx + dx, gy, gz + dy), device_id_type=MESH,
                    ),
                    in_grid(dx, dy),
                    in_grid(-dx, -dy),
                )
            )
        return made

    def start_halo(made):
        for copy, to, _ in made:
            pl.when(to)(copy.start)

    def wait_halo(made):
        for copy, to, origin in made:
            pl.when(origin)(copy.wait_recv)
        for copy, to, origin in made:
            pl.when(to)(copy.wait_send)

    h1 = halo_copies(ext, yrecv, h1_ss.at[0], h1_rs.at[0])
    start_halo(h1)

    tile = own_tile
    for n, copy in enumerate(ag1_copies):
        copy.wait_recv()
        tile = tile + ag1[n]
    ag_own[...] = tile
    ag2_copies = []
    for offset in range(1, q_count):
        copy = pltpu.make_async_remote_copy(
            src_ref=ag_own, dst_ref=cells.at[q], send_sem=ag2_ss.at[offset - 1], recv_sem=ag2_rs.at[offset - 1],
            device_id=q_peer(offset), device_id_type=MESH,
        )
        copy.start()
        ag2_copies.append(copy)
    cells[q] = tile

    def brick_transposed(base):
        return base[0, W : W + sx, 0:sy, 0:sz].reshape(sx * sy, sz).T

    f_t = brick_transposed(ext)

    for copy in ag2_copies:
        copy.wait_recv()

    listed = jnp.concatenate([cells[n] for n in range(q_count)], axis=1)
    cell_x = listed[0:1].astype(jnp.int32) - gx * sx
    cell_y = listed[1:2].astype(jnp.int32) - gz * sy
    cell_z = listed[2:3].astype(jnp.int32) - gy * sz
    area = listed[3:4]
    inside = (cell_x >= 0) & (cell_x < sx) & (cell_y >= 0) & (cell_y < sy) & (cell_z >= 0) & (cell_z < sz)
    row_id = jnp.where(inside, cell_x * sy + cell_y, -1)
    near = (cell_x >= -W) & (cell_x < sx + W) & (cell_y >= -W) & (cell_y < sy + W) & (cell_z >= -W) & (cell_z < sz + W)
    row_ext = jnp.where(near, (cell_x + W) * ey + jnp.where(cell_y < 0, cell_y + ey, cell_y), -1)

    def fill_onehot(ref, ids, block):
        def body(i, _):
            start = pl.multiple_of(i * block, block)
            sub = lax.broadcasted_iota(jnp.int32, (block, count), 0) + start
            ref[pl.ds(start, block), :] = jnp.where(sub == ids, 1.0, 0.0).astype(BF16)
            return 0

        lax.fori_loop(0, ref.shape[0] // block, body, 0)

    fill_onehot(onehot, row_id, 32)

    block_j = 512

    def gather_weights(f_t, send):
        parts = jnp.concatenate(split3(f_t), axis=0)
        pieces = []
        for start in range(0, count, block_j):
            got = jnp.dot(parts, onehot[:, start : start + block_j], preferred_element_type=F32)
            value = got[0:sz] + got[sz : 2 * sz] + got[2 * sz :]
            sub = lax.broadcasted_iota(jnp.int32, (sz, block_j), 0)
            value = jnp.where(sub == cell_z[:, start : start + block_j], value, 0.0)
            pieces.append(jnp.sum(value, axis=0, keepdims=True) * area[:, start : start + block_j])
        row = jnp.concatenate(pieces, axis=1)
        for n in range(q_count):
            send[n : n + 1, :] = row[:, n * width : (n + 1) * width]

    def w_stage2(r, copies1):
        value = ws1_send[r]
        for n, copy in enumerate(copies1):
            copy.wait_recv()
            value = value + ws1[r, n]
        ws2_send[r] = value
        copies = []
        for offset in range(1, q_count):
            copy = pltpu.make_async_remote_copy(
                src_ref=ws2_send.at[r], dst_ref=ws2.at[r, offset - 1],
                send_sem=w2_ss.at[r, offset - 1], recv_sem=w2_rs.at[r, offset - 1],
                device_id=q_peer(offset), device_id_type=MESH,
            )
            copy.start()
            copies.append(copy)
        return copies

    def w_total(r, copies2):
        value = ws2_send[r]
        for n, copy in enumerate(copies2):
            copy.wait_recv()
            value = value + ws2[r, n]
        return jnp.concatenate([value[n : n + 1] for n in range(q_count)], axis=1)

    sub8 = lax.broadcasted_iota(jnp.int32, (8, sz), 0)

    def fill_y(base, yr, arrays):
        for a in range(arrays):
            base[a, :, sy:, 0:sz] = jnp.where(sub8[None] < W, yr[0, a], yr[1, a])

    def z_copies(base, zs, zr, arrays, ss, rs):
        for a in range(arrays):
            flat = base[a, :, :, 0:sz].reshape(rows, sz)
            if rows_pad > rows:
                flat = jnp.concatenate([flat, jnp.zeros((rows_pad - rows, sz), F32)], axis=0)
            turned = flat.T
            zs[0, a] = turned[0:8]
            zs[1, a] = turned[sz - 8 :]
        made = []
        for n, step in enumerate((-1, 1)):
            to = gy > 0 if step < 0 else gy < gyn - 1
            origin = gy < gyn - 1 if step < 0 else gy > 0
            copy = pltpu.make_async_remote_copy(
                src_ref=zs.at[n], dst_ref=zr.at[n], send_sem=ss.at[n], recv_sem=rs.at[n],
                device_id=(gx, gy + step, gz), device_id_type=MESH,
            )
            made.append((copy, to, origin))
        return made

    def fill_z(base, zr, arrays):
        for a in range(arrays):
            turned = jnp.concatenate([zr[0, a], jnp.zeros((sz - 16, rows_pad), F32), zr[1, a]], axis=0)
            base[a, :, :, sz:] = turned.T[0:rows].reshape(ex, ey, sz)

    keep_k = kmat.shape[0] == count
    block_i = 32

    def kernel_block(start):
        squared = None
        for component in range(3):
            offset = cols[pl.ds(start, block_i), component : component + 1] - listed[component : component + 1]
            squared = offset * offset if squared is None else squared + offset * offset
        return lax.rsqrt(squared + 1.0)

    def potentials(weights):
        def body(i, _):
            start = pl.multiple_of(i * block_i, block_i)
            block = kmat[pl.ds(start, block_i), :] if keep_k else kernel_block(start)
            value = jnp.sum(block * weights, axis=1, keepdims=True)
            cols[pl.ds(start, block_i), 4:5] = value
            z_id = cols[pl.ds(start, block_i), 2:3].astype(jnp.int32) - gy * sz
            z_id = jnp.where(z_id < 0, z_id + ez, z_id)
            lane = lax.broadcasted_iota(jnp.int32, (block_i, ez), 1)
            placed = jnp.where(lane == z_id, value, 0.0)
            high, low = split2(placed)
            spread[pl.ds(start, block_i), 0:ez] = high
            spread[pl.ds(start, block_i), ez:] = low
            return 0

        lax.fori_loop(0, count // block_i, body, 0)

    planes = 4

    def make_load():
        def body(i, _):
            start = pl.multiple_of(i * (planes * ey), 32)
            got = jnp.dot(onehot_ext[pl.ds(start, planes * ey), :], spread[...], preferred_element_type=F32)
            got = (got[:, 0:ez] + got[:, ez:]).reshape(planes, ey, ez)
            at = pl.ds(i * planes, planes)
            load[at] = (ext[1, at] + got) * inv[at]
            return 0

        lax.fori_loop(0, ex // planes, body, 0)

    def shifted(plane):
        return (
            pltpu.roll(plane, ey - 1, 0),
            pltpu.roll(plane, 1, 0),
            pltpu.roll(plane, ez - 1, 1),
            pltpu.roll(plane, 1, 1),
        )

    def make_coefficients():
        inv[0] = jnp.zeros((ey, ez), F32)
        inv[ex - 1] = jnp.zeros((ey, ez), F32)

        def body(x, _):
            middle = ext[2, x]
            others = (ext[2, x + 1], ext[2, x - 1]) + shifted(middle)
            faces = [0.5 * (middle + other) for other in others]
            diagonal = faces[0]
            for face in faces[1:]:
                diagonal = diagonal + face
            filled = middle > 0.0
            scale = jnp.where(filled, relax / jnp.where(filled, diagonal, 1.0), 0.0)
            inv[x] = scale
            for n, face in enumerate(faces):
                coef[n, x] = face * scale
            return 0

        lax.fori_loop(1, ex - 1, body, 0)

    def sweep(read, write, first, last, brick_only):
        def body(x, _):
            plane = read(x)
            values = (read(x + 1), read(x - 1)) + shifted(plane)
            if brick_only:
                cut = lambda array: array[0:sy, 0:sz]
                new = (1.0 - relax) * cut(plane) + load[x, 0:sy, 0:sz]
                for n, value in enumerate(values):
                    new = new + coef[n, x, 0:sy, 0:sz] * cut(value)
            else:
                new = (1.0 - relax) * plane + load[x]
                for n, value in enumerate(values):
                    new = new + coef[n, x] * value
            write(x, new)
            return 0

        lax.fori_loop(first, last, body, 0)

    def sweeps(start, write_last):
        reads = [start, lambda x: ping[x], lambda x: pong[x], lambda x: ping[x]]

        def to_ping(x, new):
            ping[x] = new

        def to_pong(x, new):
            pong[x] = new

        writes = [to_ping, to_pong, to_ping, write_last]
        for s in range(SWEEPS):
            sweep(reads[s], writes[s], s + 1, ex - s - 1, s == SWEEPS - 1)

    gather_weights(f_t, ws1_send.at[0])
    w1 = exchange_z(ws1_send.at[0], ws1.at[0], w1_ss.at[0], w1_rs.at[0])
    wait_halo(h1)
    fill_y(ext, yrecv, 3)
    h2 = z_copies(ext, zsend, zrecv, 3, h2_ss.at[0], h2_rs.at[0])
    start_halo(h2)
    w2 = w_stage2(0, w1)
    for n in range(count // 128):
        wide = jnp.concatenate([listed[:, n * 128 : (n + 1) * 128], jnp.zeros((120, 128), F32)], axis=0)
        cols[n * 128 : (n + 1) * 128, :] = wide.T
    if keep_k:

        def build(i, _):
            start = pl.multiple_of(i * block_i, block_i)
            kmat[pl.ds(start, block_i), :] = kernel_block(start)
            return 0

        lax.fori_loop(0, count // block_i, build, 0)
    fill_onehot(onehot_ext, row_ext, 32)
    wait_halo(h2)
    fill_z(ext, zrecv, 3)
    make_coefficients()
    potentials(w_total(0, w2))
    make_load()

    def to_ext2(x, new):
        ext2[0, x, 0:sy, 0:sz] = new

    sweeps(lambda x: ext[0, x], to_ext2)

    h1b = halo_copies(ext2, yrecv2, h1_ss.at[1], h1_rs.at[1])
    start_halo(h1b)
    gather_weights(brick_transposed(ext2), ws1_send.at[1])
    w1b = exchange_z(ws1_send.at[1], ws1.at[1], w1_ss.at[1], w1_rs.at[1])
    wait_halo(h1b)
    fill_y(ext2, yrecv2, 1)
    h2b = z_copies(ext2, zsend2, zrecv2, 1, h2_ss.at[1], h2_rs.at[1])
    start_halo(h2b)
    w2b = w_stage2(1, w1b)
    wait_halo(h2b)
    fill_z(ext2, zrecv2, 1)
    potentials(w_total(1, w2b))
    pot_ref[...] = cols[pl.ds(pl.multiple_of((q * gzn + gz) * own, own), own), 4:5]
    make_load()

    def to_out(x, new):
        out_ref[x - W] = new

    sweeps(lambda x: ext2[0, x], to_out)

    for copy in ag1_copies + ag2_copies + w1 + w2 + w1b + w2b:
        copy.wait_send()


def shards(source, conductance, field_start, panel_cell, panel_area):
    gxn, gyn, gzn = (lax.axis_size(name) for name in ("gx", "gy", "gz"))
    sx, sy, sz = field_start.shape
    own = panel_cell.shape[1]
    q_count = gxn * gyn
    width = own * gzn
    count = width * q_count
    cfg = (gxn, gyn, gzn, sx, sy, sz, own, count)
    panel = jnp.concatenate(
        [panel_cell.astype(F32), panel_area[None, :], jnp.zeros((4, own), F32)], axis=0
    )
    panel = jnp.tile(panel, (1, gzn))
    ex, ey, ez = sx + 2 * W, sy + 8, 2 * sz
    rows = ex * ey
    rows_pad = -(-rows // 128) * 128
    vmem = pltpu.VMEM
    dma = pltpu.SemaphoreType.DMA
    k_shape = (count, count) if count <= 1024 else (8, 128)
    scratch = [
        vmem((3, ex, ey, ez), F32),
        vmem((1, ex, ey, ez), F32),
        vmem((ex, ey, ez), F32),
        vmem((ex, ey, ez), F32),
        vmem((6, ex, ey, ez), F32),
        vmem((ex, ey, ez), F32),
        vmem((ex, ey, ez), F32),
        vmem((2, 3, ex, 8, sz), F32),
        vmem((2, 1, ex, 8, sz), F32),
        vmem((2, 3, 8, rows_pad), F32),
        vmem((2, 1, 8, rows_pad), F32),
        vmem((2, 3, 8, rows_pad), F32),
        vmem((2, 1, 8, rows_pad), F32),
        vmem((8, width), F32),
        vmem((gzn - 1, 8, width), F32),
        vmem((8, width), F32),
        vmem((q_count, 8, width), F32),
        vmem((2, q_count, width), F32),
        vmem((2, gzn - 1, q_count, width), F32),
        vmem((2, q_count, width), F32),
        vmem((2, q_count - 1, q_count, width), F32),
        vmem((count, 128), F32),
        vmem((sx * sy, count), BF16),
        vmem((rows, count), BF16),
        vmem((count, 2 * ez), BF16),
        vmem(k_shape, F32),
        dma((3,)),
        dma((gzn - 1,)), dma((gzn - 1,)),
        dma((q_count - 1,)), dma((q_count - 1,)),
        dma((2, 8)), dma((2, 8)),
        dma((2, 2)), dma((2, 2)),
        dma((2, gzn - 1)), dma((2, gzn - 1)),
        dma((2, q_count - 1)), dma((2, q_count - 1)),
    ]
    whole = pl.BlockSpec(memory_space=pltpu.VMEM)
    apart = pl.BlockSpec(memory_space=pl.ANY)
    field, potential = pl.pallas_call(
        functools.partial(kernel, cfg),
        out_shape=(
            jax.ShapeDtypeStruct((sx, sy, sz), F32),
            jax.ShapeDtypeStruct((own, 1), F32),
        ),
        in_specs=[whole, apart, apart, apart],
        out_specs=(whole, whole),
        scratch_shapes=scratch,
        compiler_params=pltpu.CompilerParams(
            collective_id=0, has_side_effects=True, vmem_limit_bytes=60 * 1024 * 1024
        ),
    )(panel, field_start, source, conductance)
    return field, potential.reshape(own)


def solution(mesh):
    in_specs = (
        P("gx", "gz", "gy"),
        P("gx", "gz", "gy"),
        P("gx", "gz", "gy"),
        P(None, ("gx", "gy", "gz")),
        P(("gx", "gy", "gz")),
    )
    out_specs = (P("gx", "gz", "gy"), P(("gx", "gy", "gz")))
    return jax.shard_map(shards, mesh=mesh, in_specs=in_specs, out_specs=out_specs, check_vma=False)
```

```python
import functools

import jax
import jax.numpy as jnp
from jax import lax
from jax.experimental import pallas as pl
from jax.experimental.pallas import tpu as pltpu
from jax.sharding import PartitionSpec as P

ROUNDS = 2
SWEEPS = 4
W = SWEEPS
relax = 0.8
MESH = pl.DeviceIdType.MESH
F32 = jnp.float32
BF16 = jnp.bfloat16


def split2(value):
    high = value.astype(BF16)
    low = (value - high.astype(F32)).astype(BF16)
    return high, low


def split3(value):
    high = value.astype(BF16)
    rest = value - high.astype(F32)
    mid = rest.astype(BF16)
    low = (rest - mid.astype(F32)).astype(BF16)
    return high, mid, low


def kernel(
    cfg, panel_ref, field_ref, source_ref, cond_ref, out_ref, pot_ref,
    ext, ext2, ping, pong, coef, inv, load, yrecv, yrecv2, zsend, zsend2, zrecv, zrecv2,
    ag1_send, ag1, ag_own, cells, ws1_send, ws1, ws2_send, ws2, cols, onehot, onehot_ext, spread, kmat,
    local_sem, ag1_ss, ag1_rs, ag2_ss, ag2_rs, h1_ss, h1_rs, h2_ss, h2_rs, w1_ss, w1_rs, w2_ss, w2_rs,
):
    gxn, gyn, gzn, sx, sy, sz, own, count = cfg
    q_count = gxn * gyn
    width = own * gzn
    ex, ey, ez = sx + 2 * W, sy + 8, 2 * sz
    rows = ex * ey
    rows_pad = zsend.shape[-1]
    gx, gy, gz = lax.axis_index("gx"), lax.axis_index("gy"), lax.axis_index("gz")
    q = gx * gyn + gy

    locals_ = []
    for a, ref in enumerate((field_ref, source_ref, cond_ref)):
        copy = pltpu.make_async_copy(ref, ext.at[a, W : W + sx, 0:sy, 0:sz], local_sem.at[a])
        copy.start()
        locals_.append(copy)

    for a in range(3):
        ext[a, 0:W, :, 0:sz] = jnp.zeros((W, ey, sz), F32)
        ext[a, W + sx :, :, 0:sz] = jnp.zeros((W, ey, sz), F32)
    ext2[0, 0:W, :, 0:sz] = jnp.zeros((W, ey, sz), F32)
    ext2[0, W + sx :, :, 0:sz] = jnp.zeros((W, ey, sz), F32)
    yrecv[...] = jnp.zeros(yrecv.shape, F32)
    yrecv2[...] = jnp.zeros(yrecv2.shape, F32)
    zrecv[...] = jnp.zeros(zrecv.shape, F32)
    zrecv2[...] = jnp.zeros(zrecv2.shape, F32)

    def z_peer(offset):
        return (gx, gy, lax.rem(gz + offset, gzn))

    def q_peer(offset):
        other = lax.rem(q + offset, q_count)
        return (other // gyn, lax.rem(other, gyn), gz)

    def in_grid(dx, dy):
        ok = None
        for step, index, size in ((dx, gx, gxn), (dy, gz, gzn)):
            if step:
                test = index < size - 1 if step > 0 else index > 0
                ok = test if ok is None else jnp.logical_and(ok, test)
        return ok

    barrier = pltpu.get_barrier_semaphore()
    total = jnp.int32(gzn - 1 + q_count - 1)
    for offset in range(1, gzn):
        pl.semaphore_signal(barrier, inc=1, device_id=z_peer(offset), device_id_type=MESH)
    for offset in range(1, q_count):
        pl.semaphore_signal(barrier, inc=1, device_id=q_peer(offset), device_id_type=MESH)
    for dx in (-1, 1):
        for dy in (-1, 1):
            ok = in_grid(dx, dy)
            total = total + jnp.where(ok, 1, 0).astype(jnp.int32)

            @pl.when(ok)
            def _():
                pl.semaphore_signal(barrier, inc=1, device_id=(gx + dx, gy, gz + dy), device_id_type=MESH)

    lane_w = lax.broadcasted_iota(jnp.int32, (8, width), 1)
    mine_lanes = jnp.logical_and(lane_w >= gz * own, lane_w < (gz + 1) * own)
    own_tile = jnp.where(mine_lanes, panel_ref[...], 0.0)
    ag1_send[...] = own_tile
    pl.semaphore_wait(barrier, total)

    def exchange_z(src, dst, ss, rs):
        copies = []
        for offset in range(1, gzn):
            copy = pltpu.make_async_remote_copy(
                src_ref=src, dst_ref=dst.at[offset - 1], send_sem=ss.at[offset - 1], recv_sem=rs.at[offset - 1],
                device_id=z_peer(offset), device_id_type=MESH,
            )
            copy.start()
            copies.append(copy)
        return copies

    ag1_copies = exchange_z(ag1_send, ag1, ag1_ss, ag1_rs)
    for copy in locals_:
        copy.wait()

    directions = [(dx, dy) for dx in (-1, 0, 1) for dy in (-1, 0, 1) if dx or dy]

    def halo_copies(base, yr, ss, rs):
        made = []
        for n, (dx, dy) in enumerate(directions):
            xs = {-1: pl.ds(W, W), 0: pl.ds(W, sx), 1: pl.ds(sx, W)}[dx]
            ys = {-1: pl.ds(0, 8), 0: pl.ds(0, sy), 1: pl.ds(sy - 8, 8)}[dy]
            xd = {-1: pl.ds(W + sx, W), 0: pl.ds(W, sx), 1: pl.ds(0, W)}[dx]
            src = base.at[:, xs, ys, pl.ds(0, sz)]
            if dy == 0:
                dst = base.at[:, xd, pl.ds(0, sy), pl.ds(0, sz)]
            else:
                dst = yr.at[0 if dy < 0 else 1, :, xd]
            made.append(
                (
                    pltpu.make_async_remote_copy(
                        src_ref=src, dst_ref=dst, send_sem=ss.at[n], recv_sem=rs.at[n],
                        device_id=(gx + dx, gy, gz + dy), device_id_type=MESH,
                    ),
                    in_grid(dx, dy),
                    in_grid(-dx, -dy),
                )
            )
        return made

    def start_halo(made):
        for copy, to, _ in made:
            pl.when(to)(copy.start)

    def wait_halo(made):
        for copy, to, origin in made:
            pl.when(origin)(copy.wait_recv)
        for copy, to, origin in made:
            pl.when(to)(copy.wait_send)

    h1 = halo_copies(ext, yrecv, h1_ss.at[0], h1_rs.at[0])
    start_halo(h1)

    tile = own_tile
    for n, copy in enumerate(ag1_copies):
        copy.wait_recv()
        tile = tile + ag1[n]
    ag_own[...] = tile
    ag2_copies = []
    for offset in range(1, q_count):
        copy = pltpu.make_async_remote_copy(
            src_ref=ag_own, dst_ref=cells.at[q], send_sem=ag2_ss.at[offset - 1], recv_sem=ag2_rs.at[offset - 1],
            device_id=q_peer(offset), device_id_type=MESH,
        )
        copy.start()
        ag2_copies.append(copy)
    cells[q] = tile

    def brick_transposed(base):
        return base[0, W : W + sx, 0:sy, 0:sz].reshape(sx * sy, sz).T

    f_t = brick_transposed(ext)

    for copy in ag2_copies:
        copy.wait_recv()

    listed = jnp.concatenate([cells[n] for n in range(q_count)], axis=1)
    cell_x = listed[0:1].astype(jnp.int32) - gx * sx
    cell_y = listed[1:2].astype(jnp.int32) - gz * sy
    cell_z = listed[2:3].astype(jnp.int32) - gy * sz
    area = listed[3:4]
    inside = (cell_x >= 0) & (cell_x < sx) & (cell_y >= 0) & (cell_y < sy) & (cell_z >= 0) & (cell_z < sz)
    row_id = jnp.where(inside, cell_x * sy + cell_y, -1)
    near = (cell_x >= -W) & (cell_x < sx + W) & (cell_y >= -W) & (cell_y < sy + W) & (cell_z >= -W) & (cell_z < sz + W)
    row_ext = jnp.where(near, (cell_x + W) * ey + jnp.where(cell_y < 0, cell_y + ey, cell_y), -1)

    def fill_onehot(ref, ids, block):
        def body(i, _):
            start = pl.multiple_of(i * block, block)
            sub = lax.broadcasted_iota(jnp.int32, (block, count), 0) + start
            ref[pl.ds(start, block), :] = jnp.where(sub == ids, 1.0, 0.0).astype(BF16)
            return 0

        lax.fori_loop(0, ref.shape[0] // block, body, 0, unroll=2)

    fill_onehot(onehot, row_id, 32)

    block_j = 512

    def gather_weights(f_t, send):
        parts = jnp.concatenate(split3(f_t), axis=0)
        pieces = []
        for start in range(0, count, block_j):
            got = jnp.dot(parts, onehot[:, start : start + block_j], preferred_element_type=F32)
            value = got[0:sz] + got[sz : 2 * sz] + got[2 * sz :]
            sub = lax.broadcasted_iota(jnp.int32, (sz, block_j), 0)
            value = jnp.where(sub == cell_z[:, start : start + block_j], value, 0.0)
            pieces.append(jnp.sum(value, axis=0, keepdims=True) * area[:, start : start + block_j])
        row = jnp.concatenate(pieces, axis=1)
        for n in range(q_count):
            send[n : n + 1, :] = row[:, n * width : (n + 1) * width]

    def w_stage2(r, copies1):
        value = ws1_send[r]
        for n, copy in enumerate(copies1):
            copy.wait_recv()
            value = value + ws1[r, n]
        ws2_send[r] = value
        copies = []
        for offset in range(1, q_count):
            copy = pltpu.make_async_remote_copy(
                src_ref=ws2_send.at[r], dst_ref=ws2.at[r, offset - 1],
                send_sem=w2_ss.at[r, offset - 1], recv_sem=w2_rs.at[r, offset - 1],
                device_id=q_peer(offset), device_id_type=MESH,
            )
            copy.start()
            copies.append(copy)
        return copies

    def w_total(r, copies2):
        value = ws2_send[r]
        for n, copy in enumerate(copies2):
            copy.wait_recv()
            value = value + ws2[r, n]
        return jnp.concatenate([value[n : n + 1] for n in range(q_count)], axis=1)

    sub8 = lax.broadcasted_iota(jnp.int32, (8, sz), 0)

    def fill_y(base, yr, arrays):
        for a in range(arrays):
            base[a, :, sy:, 0:sz] = jnp.where(sub8[None] < W, yr[0, a], yr[1, a])

    def z_copies(base, zs, zr, arrays, ss, rs):
        for a in range(arrays):
            flat = base[a, :, :, 0:sz].reshape(rows, sz)
            if rows_pad > rows:
                flat = jnp.concatenate([flat, jnp.zeros((rows_pad - rows, sz), F32)], axis=0)
            turned = flat.T
            zs[0, a] = turned[0:8]
            zs[1, a] = turned[sz - 8 :]
        made = []
        for n, step in enumerate((-1, 1)):
            to = gy > 0 if step < 0 else gy < gyn - 1
            origin = gy < gyn - 1 if step < 0 else gy > 0
            copy = pltpu.make_async_remote_copy(
                src_ref=zs.at[n], dst_ref=zr.at[n], send_sem=ss.at[n], recv_sem=rs.at[n],
                device_id=(gx, gy + step, gz), device_id_type=MESH,
            )
            made.append((copy, to, origin))
        return made

    def fill_z(base, zr, arrays):
        for a in range(arrays):
            turned = jnp.concatenate([zr[0, a], jnp.zeros((sz - 16, rows_pad), F32), zr[1, a]], axis=0)
            base[a, :, :, sz:] = turned.T[0:rows].reshape(ex, ey, sz)

    keep_k = kmat.shape[0] == count
    block_i = max(16, 131072 // count)

    def kernel_block(start):
        squared = None
        for component in range(3):
            offset = cols[pl.ds(start, block_i), component : component + 1] - listed[component : component + 1]
            squared = offset * offset if squared is None else squared + offset * offset
        return lax.rsqrt(squared + 1.0)

    def potentials(weights):
        def body(i, _):
            start = pl.multiple_of(i * block_i, block_i)
            block = kmat[pl.ds(start, block_i), :] if keep_k else kernel_block(start)
            value = jnp.sum(block * weights, axis=1, keepdims=True)
            cols[pl.ds(start, block_i), 4:5] = value
            z_id = cols[pl.ds(start, block_i), 2:3].astype(jnp.int32) - gy * sz
            z_id = jnp.where(z_id < 0, z_id + ez, z_id)
            lane = lax.broadcasted_iota(jnp.int32, (block_i, ez), 1)
            placed = jnp.where(lane == z_id, value, 0.0)
            high, low = split2(placed)
            spread[pl.ds(start, block_i), 0:ez] = high
            spread[pl.ds(start, block_i), ez:] = low
            return 0

        lax.fori_loop(0, count // block_i, body, 0)

    planes = ex // 2

    def make_load():
        def body(i, _):
            start = pl.multiple_of(i * (planes * ey), 32)
            got = jnp.dot(onehot_ext[pl.ds(start, planes * ey), :], spread[...], preferred_element_type=F32)
            got = (got[:, 0:ez] + got[:, ez:]).reshape(planes, ey, ez)
            at = pl.ds(i * planes, planes)
            load[at] = (ext[1, at] + got) * inv[at]
            return 0

        lax.fori_loop(0, ex // planes, body, 0)

    def shifted(plane):
        return (
            pltpu.roll(plane, ey - 1, 0),
            pltpu.roll(plane, 1, 0),
            pltpu.roll(plane, ez - 1, 1),
            pltpu.roll(plane, 1, 1),
        )

    def make_coefficients():
        inv[0] = jnp.zeros((ey, ez), F32)
        inv[ex - 1] = jnp.zeros((ey, ez), F32)

        def body(x, _):
            middle = ext[2, x]
            others = (ext[2, x + 1], ext[2, x - 1]) + shifted(middle)
            faces = [0.5 * (middle + other) for other in others]
            diagonal = faces[0]
            for face in faces[1:]:
                diagonal = diagonal + face
            filled = middle > 0.0
            scale = jnp.where(filled, relax / jnp.where(filled, diagonal, 1.0), 0.0)
            inv[x] = scale
            for n, face in enumerate(faces):
                coef[n, x] = face * scale
            return 0

        lax.fori_loop(1, ex - 1, body, 0, unroll=2)

    def sweep(read, write, first, last, brick_only):
        def body(x, _):
            plane = read(x)
            values = (read(x + 1), read(x - 1)) + shifted(plane)
            if brick_only:
                cut = lambda array: array[0:sy, 0:sz]
                new = (1.0 - relax) * cut(plane) + load[x, 0:sy, 0:sz]
                for n, value in enumerate(values):
                    new = new + coef[n, x, 0:sy, 0:sz] * cut(value)
            else:
                new = (1.0 - relax) * plane + load[x]
                for n, value in enumerate(values):
                    new = new + coef[n, x] * value
            write(x, new)
            return 0

        lax.fori_loop(first, last, body, 0, unroll=True)

    def sweeps(start, write_last):
        reads = [start, lambda x: ping[x], lambda x: pong[x], lambda x: ping[x]]

        def to_ping(x, new):
            ping[x] = new

        def to_pong(x, new):
            pong[x] = new

        writes = [to_ping, to_pong, to_ping, write_last]
        for s in range(SWEEPS):
            sweep(reads[s], writes[s], s + 1, ex - s - 1, s == SWEEPS - 1)

    gather_weights(f_t, ws1_send.at[0])
    w1 = exchange_z(ws1_send.at[0], ws1.at[0], w1_ss.at[0], w1_rs.at[0])
    wait_halo(h1)
    fill_y(ext, yrecv, 3)
    h2 = z_copies(ext, zsend, zrecv, 3, h2_ss.at[0], h2_rs.at[0])
    start_halo(h2)
    w2 = w_stage2(0, w1)
    for n in range(count // 128):
        wide = jnp.concatenate([listed[:, n * 128 : (n + 1) * 128], jnp.zeros((120, 128), F32)], axis=0)
        cols[n * 128 : (n + 1) * 128, :] = wide.T
    if keep_k:

        def build(i, _):
            start = pl.multiple_of(i * block_i, block_i)
            kmat[pl.ds(start, block_i), :] = kernel_block(start)
            return 0

        lax.fori_loop(0, count // block_i, build, 0)
    fill_onehot(onehot_ext, row_ext, 32)
    wait_halo(h2)
    fill_z(ext, zrecv, 3)
    make_coefficients()
    potentials(w_total(0, w2))
    make_load()

    def to_ext2(x, new):
        ext2[0, x, 0:sy, 0:sz] = new

    sweeps(lambda x: ext[0, x], to_ext2)

    h1b = halo_copies(ext2, yrecv2, h1_ss.at[1], h1_rs.at[1])
    start_halo(h1b)
    gather_weights(brick_transposed(ext2), ws1_send.at[1])
    w1b = exchange_z(ws1_send.at[1], ws1.at[1], w1_ss.at[1], w1_rs.at[1])
    wait_halo(h1b)
    fill_y(ext2, yrecv2, 1)
    h2b = z_copies(ext2, zsend2, zrecv2, 1, h2_ss.at[1], h2_rs.at[1])
    start_halo(h2b)
    w2b = w_stage2(1, w1b)
    wait_halo(h2b)
    fill_z(ext2, zrecv2, 1)
    potentials(w_total(1, w2b))
    row = cols[pl.ds(pl.multiple_of(q * width, width), width), :].T[4:5]
    row = pltpu.roll(row, lax.rem(width - gz * own, width), 1)
    pot_ref[...] = row[:, 0:own]
    make_load()

    def to_out(x, new):
        out_ref[x - W] = new

    sweeps(lambda x: ext2[0, x], to_out)

    for copy in ag1_copies + ag2_copies + w1 + w2 + w1b + w2b:
        copy.wait_send()


def shards(source, conductance, field_start, panel_cell, panel_area):
    gxn, gyn, gzn = (lax.axis_size(name) for name in ("gx", "gy", "gz"))
    sx, sy, sz = field_start.shape
    own = panel_cell.shape[1]
    q_count = gxn * gyn
    width = own * gzn
    count = width * q_count
    cfg = (gxn, gyn, gzn, sx, sy, sz, own, count)
    panel = jnp.concatenate(
        [panel_cell.astype(F32), panel_area[None, :], jnp.zeros((4, own), F32)], axis=0
    )
    panel = jnp.tile(panel, (1, gzn))
    ex, ey, ez = sx + 2 * W, sy + 8, 2 * sz
    rows = ex * ey
    rows_pad = -(-rows // 128) * 128
    vmem = pltpu.VMEM
    dma = pltpu.SemaphoreType.DMA
    k_shape = (count, count) if count <= 1024 else (8, 128)
    scratch = [
        vmem((3, ex, ey, ez), F32),
        vmem((1, ex, ey, ez), F32),
        vmem((ex, ey, ez), F32),
        vmem((ex, ey, ez), F32),
        vmem((6, ex, ey, ez), F32),
        vmem((ex, ey, ez), F32),
        vmem((ex, ey, ez), F32),
        vmem((2, 3, ex, 8, sz), F32),
        vmem((2, 1, ex, 8, sz), F32),
        vmem((2, 3, 8, rows_pad), F32),
        vmem((2, 1, 8, rows_pad), F32),
        vmem((2, 3, 8, rows_pad), F32),
        vmem((2, 1, 8, rows_pad), F32),
        vmem((8, width), F32),
        vmem((gzn - 1, 8, width), F32),
        vmem((8, width), F32),
        vmem((q_count, 8, width), F32),
        vmem((2, q_count, width), F32),
        vmem((2, gzn - 1, q_count, width), F32),
        vmem((2, q_count, width), F32),
        vmem((2, q_count - 1, q_count, width), F32),
        vmem((count, 128), F32),
        vmem((sx * sy, count), BF16),
        vmem((rows, count), BF16),
        vmem((count, 2 * ez), BF16),
        vmem(k_shape, F32),
        dma((3,)),
        dma((gzn - 1,)), dma((gzn - 1,)),
        dma((q_count - 1,)), dma((q_count - 1,)),
        dma((2, 8)), dma((2, 8)),
        dma((2, 2)), dma((2, 2)),
        dma((2, gzn - 1)), dma((2, gzn - 1)),
        dma((2, q_count - 1)), dma((2, q_count - 1)),
    ]
    whole = pl.BlockSpec(memory_space=pltpu.VMEM)
    apart = pl.BlockSpec(memory_space=pl.ANY)
    field, potential = pl.pallas_call(
        functools.partial(kernel, cfg),
        out_shape=(
            jax.ShapeDtypeStruct((sx, sy, sz), F32),
            jax.ShapeDtypeStruct((1, own), F32),
        ),
        in_specs=[whole, apart, apart, apart],
        out_specs=(whole, whole),
        scratch_shapes=scratch,
        compiler_params=pltpu.CompilerParams(
            collective_id=0, has_side_effects=True, vmem_limit_bytes=60 * 1024 * 1024
        ),
    )(panel, field_start, source, conductance)
    return field, potential.reshape(own)


def solution(mesh):
    in_specs = (
        P("gx", "gz", "gy"),
        P("gx", "gz", "gy"),
        P("gx", "gz", "gy"),
        P(None, ("gx", "gy", "gz")),
        P(("gx", "gy", "gz")),
    )
    out_specs = (P("gx", "gz", "gy"), P(("gx", "gy", "gz")))
    return jax.shard_map(shards, mesh=mesh, in_specs=in_specs, out_specs=out_specs, check_vma=False)
```
